512 devices in a mesh: tp: 8 (over y, core), cp: 64 (over x, z).
Axes of the slice: x: 4, y: 4, z: 16, core: 2. Of those that a mesh axis runs over, the one named last changes fastest.
Arguments:
- features: bfloat16 [3, 8704, 8192], P(None, 'cp', 'tp'), may hold values from -6 to 6
- short_filter: float32 [3, 3, 8192], P(None, None, 'tp'), may hold values from -4 to 4
- long_filter: float32 [128, 8192], P(None, 'tp'), may hold values from -0.5 to 0.5
- skip_scale: float32 [8192], P('tp'), may hold values from -4 to 4
- out_weight: bfloat16 [8192, 8192], P('tp', 'cp'), may hold values from -0.1875 to 0.1875
Outputs:
- mixed: bfloat16 [8704, 8192], P('cp', 'tp')
The draws below stay inside these ranges and needn't reach their ends.
All inputs are finite; a program needn't handle non-finite values.
Results may differ from the reference program's by a relative error of at most 0.017.
Values may be sent and summed in bfloat16 or wider, within the bound.
No kernel may reach another device: no remote copies, remote signals or barrier semaphores. Data moves between devices by JAX's collectives and lax.ppermute only.
A program may use at most 64 MiB of HBM per device.

```python
import jax
import jax.numpy as jnp
from jax import lax

D = 8192
C = 8192
TAPS = 128
SHORT = 3
TOKENS = 8704
N_TP = 8


def spiked(array, rng, source, target, shards_of, factor):
    def block_of(dim):
        return (jnp.arange(array.shape[dim]) // (array.shape[dim] // shards_of)).reshape((-1,) + (1,) * (array.ndim - 1 - dim))

    first = jax.random.permutation(rng, shards_of)[block_of(target)]
    far = (block_of(target) + shards_of // 2) % shards_of
    return jnp.where((block_of(source) == first) | (block_of(source) == far), factor * array, array)


def levels(stream_key, dims, split, least, high):
    def one(dim, parts):
        steps = jax.random.uniform(jax.random.fold_in(jax.random.fold_in(stream_key, 6), dim), (parts,), jnp.float32, least / len(split), high / len(split))
        return jnp.repeat(jnp.exp(steps), dims[dim] // parts).reshape((-1,) + (1,) * (len(dims) - dim - 1))

    loudness = one(*split[0])
    for cut in split[1:]:
        loudness = loudness * one(*cut)
    return loudness


def bell_draw(stream_key, shape, spread, reach, split=(), kind=jnp.bfloat16):
    result = spread * jax.random.normal(stream_key, shape, jnp.float32)
    if split:
        result = result * levels(stream_key, shape, split, -0.22, 0.18)
    return jnp.clip(result, -reach, reach).astype(kind)


def bell_draw_with(own_key, dims, deviation, reach, split, heavy, kind=jnp.bfloat16):
    drawn = deviation * jax.random.normal(own_key, dims, jnp.float32)
    if split:
        drawn = drawn * levels(own_key, dims, split, -0.22, 0.18)
    return jnp.clip(spiked(drawn, jax.random.fold_in(own_key, 3), *heavy), -reach, reach).astype(kind)


def setup_inputs(seed: int = 0) -> dict:
    key_list = jax.random.split(jax.random.key(seed), 6)
    return {
        "features": bell_draw(key_list[0], (3, TOKENS, C), 1.0, 6.0, ((1, 64), (2, 8))),
        "short_filter": bell_draw(key_list[1], (3, SHORT, C), 0.6, 4.0, ((2, 8),), jnp.float32),
        "long_filter": bell_draw(key_list[2], (TAPS, C), TAPS ** -0.5, 0.5, ((1, 8),), jnp.float32),
        "skip_scale": bell_draw(key_list[3], (C,), 1.0, 4.0, ((0, 8),), jnp.float32),
        "out_weight": bell_draw_with(key_list[4], (C, D), C ** -0.5, 0.1875, ((0, 8), (1, 64)), (0, 1, 64, 4.0)),
    }


def short_conv(extended, short_filter):
    out_rows = extended.shape[1] - (SHORT - 1)
    summed = jnp.zeros((extended.shape[0], out_rows, extended.shape[2]), jnp.float32)
    for lag in range(SHORT):
        begin = SHORT - 1 - lag
        summed = summed + short_filter[:, lag, None, :] * extended[:, begin:begin + out_rows, :]
    return summed


def long_conv(product_ext, long_filter, skip_scale):
    out_rows = product_ext.shape[0] - (TAPS - 1)
    summed = skip_scale[None, :] * product_ext[TAPS - 1:]
    for lag in range(TAPS):
        begin = TAPS - 1 - lag
        summed = summed + long_filter[lag][None, :] * product_ext[begin:begin + out_rows]
    return summed


def reference(features, short_filter, long_filter, skip_scale, out_weight):
    channels = C // N_TP

    def one_group(summed, group_index):
        offset = group_index * channels
        inputs_block = lax.dynamic_slice_in_dim(features, offset, channels, 2).astype(jnp.float32)
        filter_block = lax.dynamic_slice_in_dim(short_filter, offset, channels, 2)
        long_block = lax.dynamic_slice_in_dim(long_filter, offset, channels, 1)
        skip_block = lax.dynamic_slice_in_dim(skip_scale, offset, channels, 0)
        weights = lax.dynamic_slice_in_dim(out_weight, offset, channels, 0)
        extended = jnp.pad(inputs_block, ((0, 0), (SHORT - 1, 0), (0, 0)))
        shorted = short_conv(extended, filter_block)
        product = shorted[1] * shorted[2]
        product_ext = jnp.pad(product, ((TAPS - 1, 0), (0, 0)))
        filtered = long_conv(product_ext, long_block, skip_block)
        gated = (shorted[0] * filtered).astype(jnp.bfloat16)
        partial_value = jnp.dot(gated, weights, preferred_element_type=jnp.float32).astype(jnp.bfloat16)
        partial_value = lax.optimization_barrier(partial_value).astype(jnp.float32)
        return summed + partial_value, None

    summed, _ = lax.scan(one_group, jnp.zeros((TOKENS, D), jnp.float32), jnp.arange(N_TP, dtype=jnp.int32))
    return summed.astype(jnp.bfloat16)
```

```python
import jax
import jax.numpy as jnp
from jax import lax
from jax.experimental import pallas as pl
from jax.experimental.pallas import tpu as pltpu
from jax.sharding import PartitionSpec as P

TAPS = 128
SHORT = 3
NX, NY, NZ, NC = 4, 4, 16, 2
ROWS = 136
LANES = 128
TILES = ROWS // 8
HALO = 144
BF = jnp.bfloat16
F32 = jnp.float32


def short_rows(ext, taps, i, rows):
    summed = taps[i, 0:1, :] * ext[i, 8 : 8 + rows, :]
    for lag in range(1, SHORT):
        summed = summed + taps[i, lag : lag + 1, :] * ext[i, 8 - lag : 8 - lag + rows, :]
    return summed


def pack_kernel(x_ref, taps_ref, out_ref, ext):
    ext[:, 0:8, :] = jnp.zeros((3, 8, LANES), F32)
    ext[:, 8 : 8 + ROWS, :] = x_ref[...].astype(F32)
    k = short_rows(ext, taps_ref, 1, ROWS)
    v = short_rows(ext, taps_ref, 2, ROWS)
    out_ref[0:128, :] = (k * v)[8:ROWS].astype(BF)
    row = lax.broadcasted_iota(jnp.int32, (8, LANES), 0)
    tails = [pltpu.roll(ext[i, ROWS : ROWS + 8, :], 2 + 2 * i, 0) for i in range(3)]
    tile = jnp.where(row < 2, tails[0], jnp.where(row < 4, tails[1], jnp.where(row < 6, tails[2], 0.0)))
    out_ref[128:144, :] = jnp.concatenate((tile, jnp.zeros((8, LANES), F32)), 0).astype(BF)


def conv_kernel(x_ref, halo_ref, taps_ref, long_ref, skip_ref, out_ref, ext, prod):
    tails = halo_ref[128:144, :].astype(F32)[0:8]
    for i in range(3):
        ext[i, 0:8, :] = pltpu.roll(tails, 6 - 2 * i, 0)
    ext[:, 8 : 8 + ROWS, :] = x_ref[...].astype(F32)
    k = short_rows(ext, taps_ref, 1, ROWS)
    v = short_rows(ext, taps_ref, 2, ROWS)
    prod[0:128, :] = halo_ref[0:128, :].astype(F32)
    prod[128 : 128 + ROWS, :] = k * v
    skip = skip_ref[...]
    start = tuple(skip * prod[128 + 8 * m : 136 + 8 * m, :] for m in range(TILES))

    def step(r, acc):
        acc = list(acc)
        taps = [jnp.broadcast_to(long_ref[pl.ds(8 * a + r, 1), :], (8, LANES)) for a in range(16)]
        for n in range(-15, TILES):
            part = prod[pl.ds(128 + 8 * n - r, 8), :]
            for a in range(16):
                if 0 <= n + a < TILES:
                    acc[n + a] = acc[n + a] + taps[a] * part
        return tuple(acc)

    acc = lax.fori_loop(0, 8, step, start)
    q = short_rows(ext, taps_ref, 0, ROWS)
    out_ref[...] = (q * jnp.concatenate(acc, 0)).astype(BF)


def run_pack(features, short_filter):
    return pl.pallas_call(
        pack_kernel,
        grid=(1024 // LANES,),
        in_specs=[
            pl.BlockSpec((3, ROWS, LANES), lambda i: (0, 0, i)),
            pl.BlockSpec((3, SHORT, LANES), lambda i: (0, 0, i)),
        ],
        out_specs=pl.BlockSpec((HALO, LANES), lambda i: (0, i)),
        out_shape=jax.ShapeDtypeStruct((HALO, 1024), BF),
        scratch_shapes=[pltpu.VMEM((3, 8 + ROWS, LANES), F32)],
        cost_estimate=pl.CostEstimate(flops=3000000, bytes_accessed=1200000, transcendentals=0),
        name="pack",
    )(features, short_filter)


def run_conv(features, halo, short_filter, long_filter, skip_scale):
    return pl.pallas_call(
        conv_kernel,
        grid=(1024 // LANES,),
        in_specs=[
            pl.BlockSpec((3, ROWS, LANES), lambda i: (0, 0, i)),
            pl.BlockSpec((HALO, LANES), lambda i: (0, i)),
            pl.BlockSpec((3, SHORT, LANES), lambda i: (0, 0, i)),
            pl.BlockSpec((TAPS, LANES), lambda i: (0, i)),
            pl.BlockSpec((1, LANES), lambda i: (0, i)),
        ],
        out_specs=pl.BlockSpec((ROWS, LANES), lambda i: (0, i)),
        out_shape=jax.ShapeDtypeStruct((ROWS, 1024), BF),
        scratch_shapes=[
            pltpu.VMEM((3, 8 + ROWS, LANES), F32),
            pltpu.VMEM((128 + ROWS, LANES), F32),
        ],
        cost_estimate=pl.CostEstimate(flops=36000000, bytes_accessed=2000000, transcendentals=0),
        name="conv",
    )(features, halo, short_filter, long_filter, skip_scale)


def mm_kernel(half_ref, a_ref, w_ref, out_ref):
    w = jnp.concatenate((w_ref[0], w_ref[1]), axis=1)
    c = jnp.dot(a_ref[...], w, preferred_element_type=F32)
    for m in range(NX):
        out_ref[m] = c[m * ROWS : (m + 1) * ROWS].astype(out_ref.dtype)


def run_mm(a, w, half, dtype):
    return pl.pallas_call(
        mm_kernel,
        grid_spec=pltpu.PrefetchScalarGridSpec(
            num_scalar_prefetch=1,
            grid=(4,),
            in_specs=[
                pl.BlockSpec((NX * ROWS, 1024), lambda j, h: (0, 0)),
                pl.BlockSpec((2, 1024, 128), lambda j, h: (h[0] * 4 + j, 0, 0)),
            ],
            out_specs=pl.BlockSpec((NX, ROWS, 256), lambda j, h: (0, 0, j)),
        ),
        out_shape=jax.ShapeDtypeStruct((NX, ROWS, 1024), dtype),
        cost_estimate=pl.CostEstimate(flops=1140000000, bytes_accessed=5000000, transcendentals=0),
        compiler_params=pltpu.CompilerParams(vmem_limit_bytes=32 * 1024 * 1024),
        name="mm",
    )(half, a, w)


def permute(block, axes, sizes, target):
    names = axes if len(axes) > 1 else axes[0]
    pairs = []
    for t in range(sizes[0]):
        for u in range(sizes[1]) if len(sizes) > 1 else (None,):
            if u is None:
                pairs.append((t, target(t)))
            else:
                d = target(t, u)
                pairs.append((t * sizes[1] + u, d[0] * sizes[1] + d[1]))
    return lax.ppermute(block, names, pairs)


def local(features, short_filter, long_filter, skip_scale, out_weight):
    tp, cp = lax.axis_index("tp"), lax.axis_index("cp")
    y, core = tp // NC, tp % NC

    weights = lax.all_gather(
        out_weight, "cp", axis=0, axis_index_groups=[[x * NZ + z for z in range(NZ)] for x in range(NX)]
    )

    packed = run_pack(features, short_filter)
    halo = lax.ppermute(packed, "cp", [(i, i + 1) for i in range(NX * NZ - 1)])
    gated = run_conv(features, halo, short_filter, long_filter, skip_scale[None, :])

    def from_x(shift):
        return permute(gated, ("cp",), (NX * NZ,), lambda i: (i + shift * NZ) % (NX * NZ))

    blocks = [gated, from_x(3), from_x(2), from_x(1)]
    twice = jnp.concatenate(blocks + blocks[:3], axis=0)
    a = lax.dynamic_slice_in_dim(twice, ROWS * y, NX * ROWS, 0)

    away = run_mm(a, weights, (1 - core)[None].astype(jnp.int32), BF)
    swapped = permute(away, ("tp",), (NY * NC,), lambda t: t ^ 1)
    here = run_mm(a, weights, core[None].astype(jnp.int32), F32)

    total = None
    for m in range(NX):
        piece = (here[m] + swapped[m].astype(F32)).astype(BF)

        def target(t, i, m=m):
            x, z = divmod(i, NZ)
            return x * NC + t % NC, (x + t // NC + m) % NX * NZ + z

        got = permute(piece, ("tp", "cp"), (NY * NC, NX * NZ), target).astype(F32)
        total = got if total is None else total + got
    return total.astype(BF)


def solution(mesh):
    return jax.shard_map(
        local,
        mesh=mesh,
        in_specs=(P(None, "cp", "tp"), P(None, None, "tp"), P(None, "tp"), P("tp"), P("tp", "cp")),
        out_specs=P("cp", "tp"),
        check_vma=False,
    )
```

```python
import jax
import jax.numpy as jnp
from jax import lax
from jax.experimental import pallas as pl
from jax.experimental.pallas import tpu as pltpu
from jax.sharding import PartitionSpec as P

TAPS = 128
SHORT = 3
NX, NY, NZ, NC = 4, 4, 16, 2
ROWS = 136
LANES = 128
WIDE = 256
TILES = ROWS // 8
HALO = 144
CHUNKS = ((0, 4), (4, 4))
BF = jnp.bfloat16
F32 = jnp.float32


def short_rows(ext, taps, i, first, rows):
    summed = taps[i, 0:1, :] * ext[i, first : first + rows, :]
    for lag in range(1, SHORT):
        summed = summed + taps[i, lag : lag + 1, :] * ext[i, first - lag : first - lag + rows, :]
    return summed


def pack_kernel(x_ref, taps_ref, out_ref, ext):
    ext[...] = x_ref[...].astype(F32)
    k = short_rows(ext, taps_ref, 1, 8, 128)
    v = short_rows(ext, taps_ref, 2, 8, 128)
    out_ref[0:128, :] = (k * v).astype(BF)
    row = lax.broadcasted_iota(jnp.int32, (8, WIDE), 0)
    tails = [pltpu.roll(ext[i, ROWS - 8 : ROWS, :], 2 + 2 * i, 0) for i in range(3)]
    tile = jnp.where(row < 2, tails[0], jnp.where(row < 4, tails[1], jnp.where(row < 6, tails[2], 0.0)))
    out_ref[128:144, :] = jnp.concatenate((tile, jnp.zeros((8, WIDE), F32)), 0).astype(BF)


def conv_kernel(x_ref, halo_ref, taps_ref, long_ref, skip_ref, out_ref, ext, prod):
    tails = halo_ref[128:144, :].astype(F32)[0:8]
    for i in range(3):
        ext[i, 0:8, :] = pltpu.roll(tails, 6 - 2 * i, 0)
    ext[:, 8 : 8 + ROWS, :] = x_ref[...].astype(F32)
    k = short_rows(ext, taps_ref, 1, 8, ROWS)
    v = short_rows(ext, taps_ref, 2, 8, ROWS)
    prod[0:128, :] = halo_ref[0:128, :].astype(F32)
    prod[128 : 128 + ROWS, :] = k * v
    skip = skip_ref[...]
    start = tuple(skip * prod[128 + 8 * m : 136 + 8 * m, :] for m in range(TILES))

    def step(r, acc):
        acc = list(acc)
        taps = [jnp.broadcast_to(long_ref[pl.ds(8 * a + r, 1), :], (8, LANES)) for a in range(16)]
        for n in range(-15, TILES):
            part = prod[pl.ds(128 + 8 * n - r, 8), :]
            for a in range(16):
                if 0 <= n + a < TILES:
                    acc[n + a] = acc[n + a] + taps[a] * part
        return tuple(acc)

    acc = lax.fori_loop(0, 8, step, start)
    q = short_rows(ext, taps_ref, 0, 8, ROWS)
    out_ref[...] = (q * jnp.concatenate(acc, 0)).astype(BF)


def run_pack(features, short_filter):
    return pl.pallas_call(
        pack_kernel,
        grid=(1024 // WIDE,),
        in_specs=[
            pl.BlockSpec((3, ROWS, WIDE), lambda i: (0, 0, i)),
            pl.BlockSpec((3, SHORT, WIDE), lambda i: (0, 0, i)),
        ],
        out_specs=pl.BlockSpec((HALO, WIDE), lambda i: (0, i)),
        out_shape=jax.ShapeDtypeStruct((HALO, 1024), BF),
        scratch_shapes=[pltpu.VMEM((3, ROWS, WIDE), F32)],
        cost_estimate=pl.CostEstimate(flops=3000000, bytes_accessed=6000000, transcendentals=0),
        name="pack",
    )(features, short_filter)


def run_conv(features, halo, short_filter, long_filter, skip_scale):
    return pl.pallas_call(
        conv_kernel,
        grid=(1024 // LANES,),
        in_specs=[
            pl.BlockSpec((3, ROWS, LANES), lambda i: (0, 0, i)),
            pl.BlockSpec((HALO, LANES), lambda i: (0, i)),
            pl.BlockSpec((3, SHORT, LANES), lambda i: (0, 0, i)),
            pl.BlockSpec((TAPS, LANES), lambda i: (0, i)),
            pl.BlockSpec((1, LANES), lambda i: (0, i)),
        ],
        out_specs=pl.BlockSpec((ROWS, LANES), lambda i: (0, i)),
        out_shape=jax.ShapeDtypeStruct((ROWS, 1024), BF),
        scratch_shapes=[
            pltpu.VMEM((3, 8 + ROWS, LANES), F32),
            pltpu.VMEM((128 + ROWS, LANES), F32),
        ],
        cost_estimate=pl.CostEstimate(flops=36000000, bytes_accessed=20000000, transcendentals=0),
        name="conv",
    )(features, halo, short_filter, long_filter, skip_scale)


def mm_kernel(where_ref, a_ref, w_ref, *rest):
    outs, (held, sem) = rest[:NX], rest[NX:]
    y, core = where_ref[0], where_ref[1]

    def copy(k, chunk):
        begin, size = CHUNKS[chunk]
        return pltpu.make_async_copy(
            w_ref.at[pl.ds(NZ * k + 8 * core + begin, size)], held.at[pl.ds(8 * k + begin, size)], sem.at[chunk, k]
        )

    for chunk in range(len(CHUNKS)):
        for k in range(NC):
            copy(k, chunk).start()
    for chunk, (begin, size) in enumerate(CHUNKS):
        c = None
        for k in range(NC):
            copy(k, chunk).wait()
            w = jnp.concatenate([held[8 * k + begin + i] for i in range(size)], axis=1)
            part = jnp.dot(a_ref[k], w, preferred_element_type=F32)
            c = part if c is None else c + part
        parts = [c[s * ROWS : (s + 1) * ROWS].astype(BF) for s in range(NX)]
        for row in range(NY):

            @pl.when(y == row)
            def _(row=row, parts=parts, begin=begin, size=size):
                for m in range(NX):
                    outs[m][:, 128 * begin : 128 * (begin + size)] = jnp.where(core == 0, parts[row ^ m], parts[row ^ m ^ 2])


def run_mm(where, a, w):
    vmem = pl.BlockSpec(memory_space=pltpu.VMEM)
    return pl.pallas_call(
        mm_kernel,
        in_specs=[pl.BlockSpec(memory_space=pltpu.SMEM), vmem, pl.BlockSpec(memory_space=pltpu.HBM)],
        out_specs=[vmem] * NX,
        out_shape=[jax.ShapeDtypeStruct((ROWS, 1024), BF)] * NX,
        scratch_shapes=[pltpu.VMEM((16, 1024, 128), BF), pltpu.SemaphoreType.DMA((len(CHUNKS), NC))],
        cost_estimate=pl.CostEstimate(flops=2280000000, bytes_accessed=7000000, transcendentals=0),
        compiler_params=pltpu.CompilerParams(vmem_limit_bytes=50 * 1024 * 1024),
        name="mm",
    )(where, a, w)


def permute(block, target):
    pairs = []
    for t in range(NY * NC):
        for i in range(NX * NZ):
            to = target(t // NC, t % NC, i // NZ, i % NZ)
            if to is not None:
                y, c, x, z = to
                pairs.append((t * NX * NZ + i, (y * NC + c) * NX * NZ + x * NZ + z))
    return lax.ppermute(block, ("tp", "cp"), pairs)


def local(features, short_filter, long_filter, skip_scale, out_weight):
    tp = lax.axis_index("tp")
    y, core = tp // NC, tp % NC

    groups = [
        [(gy * NC + c) * NX * NZ + gx * NZ + gz for c in range(NC) for gz in range(NZ)]
        for gy in range(NY)
        for gx in range(NX)
    ]
    weights = lax.all_gather(out_weight, ("tp", "cp"), axis=0, axis_index_groups=groups)

    packed = run_pack(features, short_filter)
    halo = lax.ppermute(packed, "cp", [(i, i + 1) for i in range(NX * NZ - 1)])
    gated = run_conv(features, halo, short_filter, long_filter, skip_scale[None, :])

    from_x = [gated] + [permute(gated, lambda y, c, x, z, s=s: (y, c, x ^ s, z)) for s in range(1, NX)]
    mine = jnp.concatenate(from_x, axis=0)
    other = permute(mine, lambda y, c, x, z: (y, 1 - c, x, z))
    a = jnp.stack((jnp.where(core == 0, mine, other), jnp.where(core == 0, other, mine)))

    pieces = run_mm(jnp.stack((y, core)).astype(jnp.int32), a, weights)
    total = None
    for m, piece in enumerate(pieces):
        got = permute(piece, lambda y, c, x, z, m=m: (x, c, x ^ y ^ m ^ (2 * c), z)).astype(F32)
        total = got if total is None else total + got
    return total.astype(BF)


def solution(mesh):
    return jax.shard_map(
        local,
        mesh=mesh,
        in_specs=(P(None, "cp", "tp"), P(None, None, "tp"), P(None, "tp"), P("tp"), P("tp", "cp")),
        out_specs=P("cp", "tp"),
        check_vma=False,
    )
```

```python
import jax
import jax.numpy as jnp
from jax import lax
from jax.experimental import pallas as pl
from jax.experimental.pallas import tpu as pltpu
from jax.sharding import PartitionSpec as P

TAPS = 128
SHORT = 3
NX, NY, NZ, NC = 4, 4, 16, 2
ROWS = 136
LANES = 128
CONV = 512
WIDE = 512
TILES = ROWS // 8
HALO = 144
ORDER = (0, 3, 1, 2)
ROUND = 60000000
OFFSETS = (0, -1, 1, -2, 2, -3, 3, -4)
BF = jnp.bfloat16
F32 = jnp.float32


def short_rows(ext, taps, i, first, rows):
    summed = taps[i, 0:1, :] * ext[i, first : first + rows, :]
    for lag in range(1, SHORT):
        summed = summed + taps[i, lag : lag + 1, :] * ext[i, first - lag : first - lag + rows, :]
    return summed


def pack_kernel(x_ref, taps_ref, out_ref, ext):
    ext[...] = x_ref[...].astype(F32)
    k = short_rows(ext, taps_ref, 1, 8, 128)
    v = short_rows(ext, taps_ref, 2, 8, 128)
    out_ref[0:128, :] = (k * v).astype(BF)
    row = lax.broadcasted_iota(jnp.int32, (8, WIDE), 0)
    tails = [pltpu.roll(ext[i, ROWS - 8 : ROWS, :], 2 + 2 * i, 0) for i in range(3)]
    tile = jnp.where(row < 2, tails[0], jnp.where(row < 4, tails[1], jnp.where(row < 6, tails[2], 0.0)))
    out_ref[128:144, :] = jnp.concatenate((tile, jnp.zeros((8, WIDE), F32)), 0).astype(BF)


def conv_kernel(x_ref, halo_ref, taps_ref, long_ref, skip_ref, out_ref, ext, prod, filt):
    def lanes(t, carry):
        here = pl.ds(pl.multiple_of(LANES * t, LANES), LANES)
        tails = halo_ref[128:144, here].astype(F32)[0:8]
        for i in range(3):
            ext[i, 0:8, :] = pltpu.roll(tails, 6 - 2 * i, 0)
            ext[i, 8 : 8 + ROWS, :] = x_ref[i, :, here].astype(F32)
        taps = taps_ref[:, :, here]
        k = short_rows(ext, taps, 1, 8, ROWS)
        v = short_rows(ext, taps, 2, 8, ROWS)
        prod[0:128, :] = halo_ref[0:128, here].astype(F32)
        prod[128 : 128 + ROWS, :] = k * v
        filt[...] = long_ref[:, here]
        skip = skip_ref[:, here]
        start = tuple(skip * prod[128 + 8 * m : 136 + 8 * m, :] for m in range(TILES))

        def step(r, acc):
            acc = list(acc)
            weights = [jnp.broadcast_to(filt[pl.ds(8 * a + r, 1), :], (8, LANES)) for a in range(16)]
            for n in range(-15, TILES):
                part = prod[pl.ds(128 + 8 * n - r, 8), :]
                for a in range(16):
                    if 0 <= n + a < TILES:
                        acc[n + a] = acc[n + a] + weights[a] * part
            return tuple(acc)

        acc = lax.fori_loop(0, 8, step, start)
        q = short_rows(ext, taps, 0, 8, ROWS)
        out_ref[:, here] = (q * jnp.concatenate(acc, 0)).astype(BF)
        return carry

    lax.fori_loop(0, CONV // LANES, lanes, 0)


def run_pack(features, short_filter):
    return pl.pallas_call(
        pack_kernel,
        grid=(1024 // WIDE,),
        in_specs=[
            pl.BlockSpec((3, ROWS, WIDE), lambda i: (0, 0, i)),
            pl.BlockSpec((3, SHORT, WIDE), lambda i: (0, 0, i)),
        ],
        out_specs=pl.BlockSpec((HALO, WIDE), lambda i: (0, i)),
        out_shape=jax.ShapeDtypeStruct((HALO, 1024), BF),
        scratch_shapes=[pltpu.VMEM((3, ROWS, WIDE), F32)],
        cost_estimate=pl.CostEstimate(flops=3000000, bytes_accessed=6000000, transcendentals=0),
        name="pack",
    )(features, short_filter)


def run_conv(features, halo, short_filter, long_filter, skip_scale):
    return pl.pallas_call(
        conv_kernel,
        grid=(1024 // CONV,),
        in_specs=[
            pl.BlockSpec((3, ROWS, CONV), lambda i: (0, 0, i)),
            pl.BlockSpec((HALO, CONV), lambda i: (0, i)),
            pl.BlockSpec((3, SHORT, CONV), lambda i: (0, 0, i)),
            pl.BlockSpec((TAPS, CONV), lambda i: (0, i)),
            pl.BlockSpec((1, CONV), lambda i: (0, i)),
        ],
        out_specs=pl.BlockSpec((ROWS, CONV), lambda i: (0, i)),
        out_shape=jax.ShapeDtypeStruct((ROWS, 1024), BF),
        scratch_shapes=[
            pltpu.VMEM((3, 8 + ROWS, LANES), F32),
            pltpu.VMEM((128 + ROWS, LANES), F32),
            pltpu.VMEM((TAPS, LANES), F32),
        ],
        cost_estimate=pl.CostEstimate(flops=36000000, bytes_accessed=20000000, transcendentals=0),
        name="conv",
    )(features, halo, short_filter, long_filter, skip_scale)


def mm_kernel(where_ref, a_ref, *rest):
    w_refs, out_ref = rest[: len(OFFSETS)], rest[len(OFFSETS)]
    rows = a_ref[...]
    for first in range(0, len(OFFSETS), 4):
        w = jnp.concatenate([w_refs[first + i][...] for i in range(4)], axis=1)
        c = jnp.dot(rows, w, preferred_element_type=F32).astype(BF)
        for i in range(4):
            column = pl.multiple_of(128 * ((where_ref[NX] + OFFSETS[first + i]) % 8), 128)
            for s in range(NX):
                out_ref[where_ref[s], :, pl.ds(column, 128)] = c[s * ROWS : (s + 1) * ROWS, 128 * i : 128 * i + 128]


def run_mm(where, a, blocks):
    vmem = pl.BlockSpec(memory_space=pltpu.VMEM)
    return pl.pallas_call(
        mm_kernel,
        in_specs=[pl.BlockSpec(memory_space=pltpu.SMEM)] + [vmem] * (1 + len(OFFSETS)),
        out_specs=vmem,
        out_shape=jax.ShapeDtypeStruct((NX, ROWS, 1024), BF),
        cost_estimate=pl.CostEstimate(flops=1140000000, bytes_accessed=5000000, transcendentals=0),
        compiler_params=pltpu.CompilerParams(vmem_limit_bytes=32 * 1024 * 1024),
        name="mm",
    )(where, a, *blocks)


def pass_kernel(*refs):
    pass


def run_pass(first, second):
    anywhere = pl.BlockSpec(memory_space=pl.ANY)
    return pl.pallas_call(
        pass_kernel,
        in_specs=[anywhere, anywhere],
        out_specs=[anywhere, anywhere],
        out_shape=[jax.ShapeDtypeStruct(first.shape, BF)] * 2,
        input_output_aliases={0: 0, 1: 1},
        cost_estimate=pl.CostEstimate(flops=1000, bytes_accessed=ROUND, transcendentals=0),
        name="hand_on",
    )(first, second)


def join_kernel(late_ref, keep_ref, other_ref, out_ref):
    late = late_ref[0] == 1
    for i in range(4):
        part = slice(128 * i, 128 * i + 128)
        keep, other = keep_ref[:, part], other_ref[:, part]
        out_ref[:, 256 * i : 256 * i + 128] = jnp.where(late, other, keep)
        out_ref[:, 256 * i + 128 : 256 * i + 256] = jnp.where(late, keep, other)


def run_join(late, keep, other):
    vmem = pl.BlockSpec(memory_space=pltpu.VMEM)
    return pl.pallas_call(
        join_kernel,
        in_specs=[pl.BlockSpec(memory_space=pltpu.SMEM), vmem, vmem],
        out_specs=vmem,
        out_shape=jax.ShapeDtypeStruct((ROWS, 1024), BF),
        cost_estimate=pl.CostEstimate(flops=1000, bytes_accessed=600000, transcendentals=0),
        name="join",
    )(late, keep, other)


def permute(block, target):
    pairs = []
    for t in range(NY * NC):
        for i in range(NX * NZ):
            to = target(t // NC, t % NC, i // NZ, i % NZ)
            if to is not None:
                y, c, x, z = to
                pairs.append((t * NX * NZ + i, (y * NC + c) * NX * NZ + x * NZ + z))
    return lax.ppermute(block, ("tp", "cp"), pairs)


def local(features, short_filter, long_filter, skip_scale, out_weight):
    tp, cp = lax.axis_index("tp"), lax.axis_index("cp")
    y, core, z = tp // NC, tp % NC, cp % NZ

    blocks = [out_weight]
    behind = ahead = out_weight
    for r in range(1, 5):
        behind = permute(behind, lambda y, c, x, z: (y, c, x, (z + 2) % NZ))
        if r < 4:
            ahead = permute(ahead, lambda y, c, x, z: (y, c, x, (z - 2) % NZ))
            behind, ahead = run_pass(behind, ahead)
            blocks += [behind, ahead]
    blocks.append(behind)

    packed = run_pack(features, short_filter)
    halo = lax.ppermute(packed, "cp", [(i, i + 1) for i in range(NX * NZ - 1)])
    gated = run_conv(features, halo, short_filter, long_filter, skip_scale[None, :])

    across = permute(gated, lambda y, c, x, z: (y, c, x, z ^ 1))

    def from_x(block):
        others = [
            permute(block, lambda y, c, x, z, i=i: (y, c, x ^ (ORDER[i] if c else i), z)) for i in range(1, NX)
        ]
        return jnp.concatenate([block] + others, axis=0)

    core, y = core.astype(jnp.int32), y.astype(jnp.int32)
    sources = jnp.where(core == 1, jnp.array(ORDER, jnp.int32), jnp.arange(NX, dtype=jnp.int32)) ^ y
    column = (z // 2).astype(jnp.int32)[None]
    near = run_mm(jnp.concatenate((sources, column)), from_x(gated), blocks)
    far = run_mm(jnp.concatenate((sources ^ 2, column)), from_x(across), blocks)

    away = permute(jnp.where(core == 0, far, near), lambda y, c, x, z: (y, 1 - c, x, z))
    keep = jnp.where(core == 0, near, far)
    got = []
    for m in range(NX):
        piece = (keep[m].astype(F32) + away[m].astype(F32)).astype(BF)
        got.append(permute(piece, lambda y, c, x, z, m=m: (x, c, x ^ y ^ m ^ (2 * c), z ^ c)))

    def half(start):
        part = [lax.dynamic_slice_in_dim(g, start, 512, 1).astype(F32) for g in got]
        return ((part[0] + part[1]) + (part[2] + part[3])).astype(BF)

    away = half(512 * (1 - core))
    other = permute(away, lambda y, c, x, z: (y, 1 - c, x, z))
    keep = half(512 * core)
    late = (z % 2) ^ core
    return run_join(late.astype(jnp.int32)[None], keep, other)


def solution(mesh):
    return jax.shard_map(
        local,
        mesh=mesh,
        in_specs=(P(None, "cp", "tp"), P(None, None, "tp"), P(None, "tp"), P("tp"), P("tp", "cp")),
        out_specs=P("cp", "tp"),
        check_vma=False,
    )
```

```python
import jax
import jax.numpy as jnp
from jax import lax
from jax.experimental import pallas as pl
from jax.experimental.pallas import tpu as pltpu
from jax.sharding import PartitionSpec as P

TAPS = 128
SHORT = 3
NX, NY, NZ, NC = 4, 4, 16, 2
ROWS = 136
LANES = 128
CONV = 512
WIDE = 512
TILES = ROWS // 8
HALO = 144
ORDER = (0, 2, 3, 1)
ROUND = 60000000
OFFSETS = (0, -1, 1, -2, 2, -3, 3, -4)
BF = jnp.bfloat16
F32 = jnp.float32


def short_rows(ext, taps, i, first, rows):
    summed = taps[i, 0:1, :] * ext[i, first : first + rows, :]
    for lag in range(1, SHORT):
        summed = summed + taps[i, lag : lag + 1, :] * ext[i, first - lag : first - lag + rows, :]
    return summed


def pack_kernel(x_ref, taps_ref, out_ref, ext):
    ext[...] = x_ref[...].astype(F32)
    k = short_rows(ext, taps_ref, 1, 8, 128)
    v = short_rows(ext, taps_ref, 2, 8, 128)
    out_ref[0:128, :] = (k * v).astype(BF)
    row = lax.broadcasted_iota(jnp.int32, (8, WIDE), 0)
    tails = [pltpu.roll(ext[i, ROWS - 8 : ROWS, :], 2 + 2 * i, 0) for i in range(3)]
    tile = jnp.where(row < 2, tails[0], jnp.where(row < 4, tails[1], jnp.where(row < 6, tails[2], 0.0)))
    out_ref[128:144, :] = jnp.concatenate((tile, jnp.zeros((8, WIDE), F32)), 0).astype(BF)


def conv_kernel(x_ref, halo_ref, taps_ref, long_ref, skip_ref, out_ref, ext, prod, filt):
    def lanes(t, carry):
        here = pl.ds(pl.multiple_of(LANES * t, LANES), LANES)
        tails = halo_ref[128:144, here].astype(F32)[0:8]
        for i in range(3):
            ext[i, 0:8, :] = pltpu.roll(tails, 6 - 2 * i, 0)
            ext[i, 8 : 8 + ROWS, :] = x_ref[i, :, here].astype(F32)
        taps = taps_ref[:, :, here]
        k = short_rows(ext, taps, 1, 8, ROWS)
        v = short_rows(ext, taps, 2, 8, ROWS)
        prod[0:128, :] = halo_ref[0:128, here].astype(F32)
        prod[128 : 128 + ROWS, :] = k * v
        filt[...] = long_ref[:, here]
        skip = skip_ref[:, here]
        start = tuple(skip * prod[128 + 8 * m : 136 + 8 * m, :] for m in range(TILES))

        def step(r, acc):
            acc = list(acc)
            weights = [jnp.broadcast_to(filt[pl.ds(8 * a + r, 1), :], (8, LANES)) for a in range(16)]
            for n in range(-15, TILES):
                part = prod[pl.ds(128 + 8 * n - r, 8), :]
                for a in range(16):
                    if 0 <= n + a < TILES:
                        acc[n + a] = acc[n + a] + weights[a] * part
            return tuple(acc)

        acc = lax.fori_loop(0, 8, step, start)
        q = short_rows(ext, taps, 0, 8, ROWS)
        out_ref[:, here] = (q * jnp.concatenate(acc, 0)).astype(BF)
        return carry

    lax.fori_loop(0, CONV // LANES, lanes, 0)


def run_pack(features, short_filter):
    return pl.pallas_call(
        pack_kernel,
        grid=(1024 // WIDE,),
        in_specs=[
            pl.BlockSpec((3, ROWS, WIDE), lambda i: (0, 0, i)),
            pl.BlockSpec((3, SHORT, WIDE), lambda i: (0, 0, i)),
        ],
        out_specs=pl.BlockSpec((HALO, WIDE), lambda i: (0, i)),
        out_shape=jax.ShapeDtypeStruct((HALO, 1024), BF),
        scratch_shapes=[pltpu.VMEM((3, ROWS, WIDE), F32)],
        cost_estimate=pl.CostEstimate(flops=3000000, bytes_accessed=6000000, transcendentals=0),
        name="pack",
    )(features, short_filter)


def run_conv(features, halo, short_filter, long_filter, skip_scale):
    return pl.pallas_call(
        conv_kernel,
        grid=(1024 // CONV,),
        in_specs=[
            pl.BlockSpec((3, ROWS, CONV), lambda i: (0, 0, i)),
            pl.BlockSpec((HALO, CONV), lambda i: (0, i)),
            pl.BlockSpec((3, SHORT, CONV), lambda i: (0, 0, i)),
            pl.BlockSpec((TAPS, CONV), lambda i: (0, i)),
            pl.BlockSpec((1, CONV), lambda i: (0, i)),
        ],
        out_specs=pl.BlockSpec((ROWS, CONV), lambda i: (0, i)),
        out_shape=jax.ShapeDtypeStruct((ROWS, 1024), BF),
        scratch_shapes=[
            pltpu.VMEM((3, 8 + ROWS, LANES), F32),
            pltpu.VMEM((128 + ROWS, LANES), F32),
            pltpu.VMEM((TAPS, LANES), F32),
        ],
        cost_estimate=pl.CostEstimate(flops=36000000, bytes_accessed=20000000, transcendentals=0),
        name="conv",
    )(features, halo, short_filter, long_filter, skip_scale)


def mm_kernel(where_ref, a_ref, *rest):
    w_refs, out_ref = rest[: len(OFFSETS)], rest[len(OFFSETS)]
    rows = a_ref[...]
    for first in range(0, len(OFFSETS), 4):
        w = jnp.concatenate([w_refs[first + i][...] for i in range(4)], axis=1)
        c = jnp.dot(rows, w, preferred_element_type=F32).astype(BF)
        for i in range(4):
            column = pl.multiple_of(128 * ((where_ref[NX] + OFFSETS[first + i]) % 8), 128)
            for s in range(NX):
                out_ref[where_ref[s], :, pl.ds(column, 128)] = c[s * ROWS : (s + 1) * ROWS, 128 * i : 128 * i + 128]


def run_mm(where, a, blocks):
    vmem = pl.BlockSpec(memory_space=pltpu.VMEM)
    return pl.pallas_call(
        mm_kernel,
        in_specs=[pl.BlockSpec(memory_space=pltpu.SMEM)] + [vmem] * (1 + len(OFFSETS)),
        out_specs=vmem,
        out_shape=jax.ShapeDtypeStruct((NX, ROWS, 1024), BF),
        cost_estimate=pl.CostEstimate(flops=1140000000, bytes_accessed=5000000, transcendentals=0),
        compiler_params=pltpu.CompilerParams(vmem_limit_bytes=32 * 1024 * 1024),
        name="mm",
    )(where, a, *blocks)


def pass_kernel(*refs):
    pass


def run_pass(first, second):
    anywhere = pl.BlockSpec(memory_space=pl.ANY)
    return pl.pallas_call(
        pass_kernel,
        in_specs=[anywhere, anywhere],
        out_specs=[anywhere, anywhere],
        out_shape=[jax.ShapeDtypeStruct(first.shape, BF)] * 2,
        input_output_aliases={0: 0, 1: 1},
        cost_estimate=pl.CostEstimate(flops=1000, bytes_accessed=ROUND, transcendentals=0),
        name="hand_on",
    )(first, second)


def join_kernel(late_ref, keep_ref, other_ref, out_ref):
    late = late_ref[0] == 1
    for i in range(4):
        part = slice(128 * i, 128 * i + 128)
        keep, other = keep_ref[:, part], other_ref[:, part]
        out_ref[:, 256 * i : 256 * i + 128] = jnp.where(late, other, keep)
        out_ref[:, 256 * i + 128 : 256 * i + 256] = jnp.where(late, keep, other)


def run_join(late, keep, other):
    vmem = pl.BlockSpec(memory_space=pltpu.VMEM)
    return pl.pallas_call(
        join_kernel,
        in_specs=[pl.BlockSpec(memory_space=pltpu.SMEM), vmem, vmem],
        out_specs=vmem,
        out_shape=jax.ShapeDtypeStruct((ROWS, 1024), BF),
        cost_estimate=pl.CostEstimate(flops=1000, bytes_accessed=600000, transcendentals=0),
        name="join",
    )(late, keep, other)


def permute(block, target):
    pairs = []
    for t in range(NY * NC):
        for i in range(NX * NZ):
            to = target(t // NC, t % NC, i // NZ, i % NZ)
            if to is not None:
                y, c, x, z = to
                pairs.append((t * NX * NZ + i, (y * NC + c) * NX * NZ + x * NZ + z))
    return lax.ppermute(block, ("tp", "cp"), pairs)


def local(features, short_filter, long_filter, skip_scale, out_weight):
    tp, cp = lax.axis_index("tp"), lax.axis_index("cp")
    y, core, z = tp // NC, tp % NC, cp % NZ

    blocks = [out_weight]
    behind = ahead = out_weight
    for r in range(1, 5):
        behind = permute(behind, lambda y, c, x, z: (y, c, x, (z + 2) % NZ))
        if r < 4:
            ahead = permute(ahead, lambda y, c, x, z: (y, c, x, (z - 2) % NZ))
            behind, ahead = run_pass(behind, ahead)
            blocks += [behind, ahead]
    blocks.append(behind)

    packed = run_pack(features, short_filter)
    halo = lax.ppermute(packed, "cp", [(i, i + 1) for i in range(NX * NZ - 1)])
    gated = run_conv(features, halo, short_filter, long_filter, skip_scale[None, :])

    across = permute(gated, lambda y, c, x, z: (y, c, x, z ^ 1))

    def from_x(block):
        others = [
            permute(block, lambda y, c, x, z, i=i: (y, c, x ^ (ORDER[i] if c else i), z)) for i in range(1, NX)
        ]
        return jnp.concatenate([block] + others, axis=0)

    core, y = core.astype(jnp.int32), y.astype(jnp.int32)
    sources = jnp.where(core == 1, jnp.array(ORDER, jnp.int32), jnp.arange(NX, dtype=jnp.int32)) ^ y
    column = (z // 2).astype(jnp.int32)[None]
    near = run_mm(jnp.concatenate((sources, column)), from_x(gated), blocks)
    far = run_mm(jnp.concatenate((sources ^ 2, column)), from_x(across), blocks)

    away = permute(jnp.where(core == 0, far, near), lambda y, c, x, z: (y, 1 - c, x, z))
    keep = jnp.where(core == 0, near, far)
    got = []
    for m in range(NX):
        piece = (keep[m].astype(F32) + away[m].astype(F32)).astype(BF)
        got.append(permute(piece, lambda y, c, x, z, m=m: (x, c, x ^ y ^ m ^ (2 * c), z ^ c)))

    def half(start):
        part = [lax.dynamic_slice_in_dim(g, start, 512, 1).astype(F32) for g in got]
        return ((part[0] + part[1]) + (part[2] + part[3])).astype(BF)

    away = half(512 * (1 - core))
    other = permute(away, lambda y, c, x, z: (y, 1 - c, x, z))
    keep = half(512 * core)
    late = (z % 2) ^ core
    return run_join(late.astype(jnp.int32)[None], keep, other)


def solution(mesh):
    return jax.shard_map(
        local,
        mesh=mesh,
        in_specs=(P(None, "cp", "tp"), P(None, None, "tp"), P(None, "tp"), P("tp"), P("tp", "cp")),
        out_specs=P("cp", "tp"),
        check_vma=False,
    )
```

```python
import jax
import jax.numpy as jnp
from jax import lax
from jax.experimental import pallas as pl
from jax.experimental.pallas import tpu as pltpu
from jax.sharding import PartitionSpec as P

TAPS = 128
SHORT = 3
NX, NY, NZ, NC = 4, 4, 16, 2
ROWS = 136
LANES = 128
CONV = 512
WIDE = 512
TILES = ROWS // 8
HALO = 144
ORDER = (0, 3, 1, 2)
ROUND = 60000000
OFFSETS = (0, -1, 1, -2, 2, -3, 3, -4)
BF = jnp.bfloat16
F32 = jnp.float32


def short_rows(ext, taps, i, first, rows):
    summed = taps[i, 0:1, :] * ext[i, first : first + rows, :]
    for lag in range(1, SHORT):
        summed = summed + taps[i, lag : lag + 1, :] * ext[i, first - lag : first - lag + rows, :]
    return summed


def pack_kernel(x_ref, taps_ref, out_ref, ext):
    ext[...] = x_ref[...].astype(F32)
    k = short_rows(ext, taps_ref, 1, 8, 128)
    v = short_rows(ext, taps_ref, 2, 8, 128)
    out_ref[0:128, :] = (k * v).astype(BF)
    row = lax.broadcasted_iota(jnp.int32, (8, WIDE), 0)
    tails = [pltpu.roll(ext[i, ROWS - 8 : ROWS, :], 2 + 2 * i, 0) for i in range(3)]
    tile = jnp.where(row < 2, tails[0], jnp.where(row < 4, tails[1], jnp.where(row < 6, tails[2], 0.0)))
    out_ref[128:144, :] = jnp.concatenate((tile, jnp.zeros((8, WIDE), F32)), 0).astype(BF)


def conv_kernel(x_ref, halo_ref, taps_ref, long_ref, skip_ref, out_ref, ext, prod, filt):
    def lanes(t, carry):
        here = pl.ds(pl.multiple_of(LANES * t, LANES), LANES)
        tails = halo_ref[128:144, here].astype(F32)[0:8]
        for i in range(3):
            ext[i, 0:8, :] = pltpu.roll(tails, 6 - 2 * i, 0)
            ext[i, 8 : 8 + ROWS, :] = x_ref[i, :, here].astype(F32)
        taps = taps_ref[:, :, here]
        k = short_rows(ext, taps, 1, 8, ROWS)
        v = short_rows(ext, taps, 2, 8, ROWS)
        prod[0:128, :] = halo_ref[0:128, here].astype(F32)
        prod[128 : 128 + ROWS, :] = k * v
        filt[...] = long_ref[:, here]
        skip = skip_ref[:, here]
        start = tuple(skip * prod[128 + 8 * m : 136 + 8 * m, :] for m in range(TILES))

        def step(r, acc):
            acc = list(acc)
            weights = [jnp.broadcast_to(filt[pl.ds(8 * a + r, 1), :], (8, LANES)) for a in range(16)]
            for n in range(-15, TILES):
                part = prod[pl.ds(128 + 8 * n - r, 8), :]
                for a in range(16):
                    if 0 <= n + a < TILES:
                        acc[n + a] = acc[n + a] + weights[a] * part
            return tuple(acc)

        acc = lax.fori_loop(0, 8, step, start)
        q = short_rows(ext, taps, 0, 8, ROWS)
        out_ref[:, here] = (q * jnp.concatenate(acc, 0)).astype(BF)
        return carry

    lax.fori_loop(0, CONV // LANES, lanes, 0)


def run_pack(features, short_filter):
    return pl.pallas_call(
        pack_kernel,
        grid=(1024 // WIDE,),
        in_specs=[
            pl.BlockSpec((3, ROWS, WIDE), lambda i: (0, 0, i)),
            pl.BlockSpec((3, SHORT, WIDE), lambda i: (0, 0, i)),
        ],
        out_specs=pl.BlockSpec((HALO, WIDE), lambda i: (0, i)),
        out_shape=jax.ShapeDtypeStruct((HALO, 1024), BF),
        scratch_shapes=[pltpu.VMEM((3, ROWS, WIDE), F32)],
        cost_estimate=pl.CostEstimate(flops=3000000, bytes_accessed=6000000, transcendentals=0),
        name="pack",
    )(features, short_filter)


def run_conv(features, halo, short_filter, long_filter, skip_scale):
    return pl.pallas_call(
        conv_kernel,
        grid=(1024 // CONV,),
        in_specs=[
            pl.BlockSpec((3, ROWS, CONV), lambda i: (0, 0, i)),
            pl.BlockSpec((HALO, CONV), lambda i: (0, i)),
            pl.BlockSpec((3, SHORT, CONV), lambda i: (0, 0, i)),
            pl.BlockSpec((TAPS, CONV), lambda i: (0, i)),
            pl.BlockSpec((1, CONV), lambda i: (0, i)),
        ],
        out_specs=pl.BlockSpec((ROWS, CONV), lambda i: (0, i)),
        out_shape=jax.ShapeDtypeStruct((ROWS, 1024), BF),
        scratch_shapes=[
            pltpu.VMEM((3, 8 + ROWS, LANES), F32),
            pltpu.VMEM((128 + ROWS, LANES), F32),
            pltpu.VMEM((TAPS, LANES), F32),
        ],
        cost_estimate=pl.CostEstimate(flops=36000000, bytes_accessed=20000000, transcendentals=0),
        name="conv",
    )(features, halo, short_filter, long_filter, skip_scale)


def mm_kernel(where_ref, a_ref, *rest):
    w_refs, out_ref = rest[: len(OFFSETS)], rest[len(OFFSETS)]
    rows = a_ref[...]
    for first in range(0, len(OFFSETS), 4):
        w = jnp.concatenate([w_refs[first + i][...] for i in range(4)], axis=1)
        c = jnp.dot(rows, w, preferred_element_type=F32).astype(BF)
        for i in range(4):
            column = pl.multiple_of(128 * ((where_ref[NX] + OFFSETS[first + i]) % 8), 128)
            for s in range(NX):
                out_ref[where_ref[s], :, pl.ds(column, 128)] = c[s * ROWS : (s + 1) * ROWS, 128 * i : 128 * i + 128]


def run_mm(where, a, blocks):
    vmem = pl.BlockSpec(memory_space=pltpu.VMEM)
    return pl.pallas_call(
        mm_kernel,
        in_specs=[pl.BlockSpec(memory_space=pltpu.SMEM)] + [vmem] * (1 + len(OFFSETS)),
        out_specs=vmem,
        out_shape=jax.ShapeDtypeStruct((NX, ROWS, 1024), BF),
        cost_estimate=pl.CostEstimate(flops=1140000000, bytes_accessed=5000000, transcendentals=0),
        compiler_params=pltpu.CompilerParams(vmem_limit_bytes=32 * 1024 * 1024),
        name="mm",
    )(where, a, *blocks)


def pass_kernel(*refs):
    pass


def run_pass(first, second):
    anywhere = pl.BlockSpec(memory_space=pl.ANY)
    return pl.pallas_call(
        pass_kernel,
        in_specs=[anywhere, anywhere],
        out_specs=[anywhere, anywhere],
        out_shape=[jax.ShapeDtypeStruct(first.shape, BF)] * 2,
        input_output_aliases={0: 0, 1: 1},
        cost_estimate=pl.CostEstimate(flops=1000, bytes_accessed=ROUND, transcendentals=0),
        name="hand_on",
    )(first, second)


def join_kernel(late_ref, keep_ref, other_ref, out_ref):
    late = late_ref[0] == 1
    for i in range(4):
        part = slice(128 * i, 128 * i + 128)
        keep, other = keep_ref[:, part], other_ref[:, part]
        out_ref[:, 256 * i : 256 * i + 128] = jnp.where(late, other, keep)
        out_ref[:, 256 * i + 128 : 256 * i + 256] = jnp.where(late, keep, other)


def run_join(late, keep, other):
    vmem = pl.BlockSpec(memory_space=pltpu.VMEM)
    return pl.pallas_call(
        join_kernel,
        in_specs=[pl.BlockSpec(memory_space=pltpu.SMEM), vmem, vmem],
        out_specs=vmem,
        out_shape=jax.ShapeDtypeStruct((ROWS, 1024), BF),
        cost_estimate=pl.CostEstimate(flops=1000, bytes_accessed=600000, transcendentals=0),
        compiler_params=pltpu.CompilerParams(vmem_limit_bytes=56 * 1024 * 1024),
        name="join",
    )(late, keep, other)


def permute(block, target):
    pairs = []
    for t in range(NY * NC):
        for i in range(NX * NZ):
            to = target(t // NC, t % NC, i // NZ, i % NZ)
            if to is not None:
                y, c, x, z = to
                pairs.append((t * NX * NZ + i, (y * NC + c) * NX * NZ + x * NZ + z))
    return lax.ppermute(block, ("tp", "cp"), pairs)


def local(features, short_filter, long_filter, skip_scale, out_weight):
    tp, cp = lax.axis_index("tp"), lax.axis_index("cp")
    y, core, z = tp // NC, tp % NC, cp % NZ

    blocks = [out_weight]
    behind = ahead = out_weight
    for r in range(1, 5):
        behind = permute(behind, lambda y, c, x, z: (y, c, x, (z + 2) % NZ))
        if r < 4:
            ahead = permute(ahead, lambda y, c, x, z: (y, c, x, (z - 2) % NZ))
            behind, ahead = run_pass(behind, ahead)
            blocks += [behind, ahead]
    blocks.append(behind)

    packed = run_pack(features, short_filter)
    halo = lax.ppermute(packed, "cp", [(i, i + 1) for i in range(NX * NZ - 1)])
    gated = run_conv(features, halo, short_filter, long_filter, skip_scale[None, :])

    across = permute(gated, lambda y, c, x, z: (y, c, x, z ^ 1))

    def from_x(block):
        others = [
            permute(block, lambda y, c, x, z, i=i: (y, c, x ^ (ORDER[i] if c else i), z)) for i in range(1, NX)
        ]
        return jnp.concatenate([block] + others, axis=0)

    core, y = core.astype(jnp.int32), y.astype(jnp.int32)
    sources = jnp.where(core == 1, jnp.array(ORDER, jnp.int32), jnp.arange(NX, dtype=jnp.int32)) ^ y
    column = (z // 2).astype(jnp.int32)[None]
    near = run_mm(jnp.concatenate((sources, column)), from_x(gated), blocks)
    far = run_mm(jnp.concatenate((sources ^ 2, column)), from_x(across), blocks)

    away = permute(jnp.where(core == 0, far, near), lambda y, c, x, z: (y, 1 - c, x, z))
    keep = jnp.where(core == 0, near, far)
    got = []
    for m in range(NX):
        piece = (keep[m].astype(F32) + away[m].astype(F32)).astype(BF)
        got.append(permute(piece, lambda y, c, x, z, m=m: (x, c, x ^ y ^ m ^ (2 * c), z ^ c)))

    def half(start):
        part = [lax.dynamic_slice_in_dim(g, start, 512, 1).astype(F32) for g in got]
        return ((part[0] + part[1]) + (part[2] + part[3])).astype(BF)

    away = half(512 * (1 - core))
    other = permute(away, lambda y, c, x, z: (y, 1 - c, x, z))
    keep = half(512 * core)
    late = (z % 2) ^ core
    return run_join(late.astype(jnp.int32)[None], keep, other)


def solution(mesh):
    return jax.shard_map(
        local,
        mesh=mesh,
        in_specs=(P(None, "cp", "tp"), P(None, None, "tp"), P(None, "tp"), P("tp"), P("tp", "cp")),
        out_specs=P("cp", "tp"),
        check_vma=False,
    )
```
